1024 devices in a mesh: expert: 64 (over x_lo, z, core), mp: 16 (over x_hi, y).
Axes of the slice: x: 8 (x_hi: 2, x_lo: 4; x = x_hi * 4 + x_lo), y: 8, z: 8, core: 2. Of those that a mesh axis runs over, the one named last changes fastest.
Arguments:
- tokens: bfloat16 [8192, 2048], P('expert', 'mp'), may hold values from -6 to 6
- cotangent: bfloat16 [8192, 2048], P('expert', 'mp'), may hold values from -6 to 6
- expert_ids: int32 [8192], P('expert'), may hold values from 0 to 63, as said below
- slots: int32 [8192], P('expert'), may hold values from -1 to 3, as said below
- gate: float32 [8192], P('expert'), may hold values from 0.1 to 1
- w_in: bfloat16 [64, 2048, 6144], P('expert', None, 'mp'), may hold values from -0.125 to 0.125
- w_out: bfloat16 [64, 6144, 2048], P('expert', 'mp'), may hold values from -0.078125 to 0.078125
Outputs:
- input_grad: bfloat16 [8192, 2048], P('expert', 'mp')
The draws below stay inside these ranges and needn't reach their ends.
Inputs may be any that keep to these rules, and one draw needn't show every extreme that they name: `expert_ids`: some expert receives exactly 4 kept tokens from every group of 128 tokens. `slots`: A kept token's slot is the number of earlier tokens of its group routed to the same expert; a token with 4 or more such earlier tokens has slot -1.
All inputs are finite; a program needn't handle non-finite values.
Results may differ from the reference program's by a relative error of at most 0.0057.
Values may be sent and summed in bfloat16 or wider, within the bound.
A program may use at most 32 MiB of HBM per device.

```python
import jax
import jax.numpy as jnp
from jax import lax

D = 2048
FF = 6144
TOK_DEV = 128
EXPERTS = 64
CAP = 4
TOKENS = 8192


def routing(key):
    groups = TOKENS // TOK_DEV
    key_list = jax.random.split(key, 5)
    draw_one = jax.random.randint(key_list[0], (groups, TOK_DEV), 0, EXPERTS)
    draw_two = jax.random.randint(key_list[1], (groups, TOK_DEV), 0, EXPERTS)
    relabel = jax.random.permutation(key_list[2], EXPERTS)
    chosen = relabel[jnp.minimum(draw_one, draw_two)]
    favored = jax.random.randint(key_list[3], (), 0, EXPERTS)

    def permute_row(row_key):
        return jax.random.permutation(row_key, TOK_DEV)
    shuffle = jax.vmap(permute_row)(jax.random.split(key_list[4], groups))
    chosen = jnp.where(shuffle < CAP + 1, favored, chosen)
    onehot = (chosen[:, :, None] == jnp.arange(EXPERTS)[None, None, :]).astype(jnp.int32)
    before = jnp.cumsum(onehot, axis=1) - onehot
    place_rank = jnp.sum(before * onehot, axis=2)
    slot_index = jnp.where(place_rank < CAP, place_rank, -1)
    return (chosen.reshape(TOKENS).astype(jnp.int32), slot_index.reshape(TOKENS).astype(jnp.int32))


def draw_expert_ids(key, part):
    return routing(key)[0]


def draw_slots(key, part):
    return routing(key)[1]


def level_of(rng, dims, shards, low, largest):
    def one(dim, parts):
        steps = jax.random.uniform(jax.random.fold_in(jax.random.fold_in(rng, 6), dim), (parts,), jnp.float32, low / len(shards), largest / len(shards))
        return jnp.repeat(jnp.exp(steps), dims[dim] // parts).reshape((-1,) + (1,) * (len(dims) - dim - 1))

    gain = one(*shards[0])
    for cut in shards[1:]:
        gain = gain * one(*cut)
    return gain


def scatter_about(rng, extent, deviation, bound, cuts=(), kind=jnp.bfloat16):
    drawn = jax.random.normal(rng, extent, jnp.float32) * deviation
    if len(cuts) > 0:
        drawn = level_of(rng, extent, cuts, -0.22, 0.18) * drawn
    return jnp.clip(drawn, min=-bound, max=bound).astype(kind)


def setup_inputs(seed: int = 0) -> dict:
    streams_of = jax.random.split(jax.random.key(seed), 8)
    return {
        "tokens": scatter_about(streams_of[0], (TOKENS, D), 1.0, 6.0, ((0, 64), (1, 16))),
        "cotangent": scatter_about(streams_of[1], (TOKENS, D), 1.0, 6.0, ((0, 64), (1, 16))),
        "expert_ids": draw_expert_ids(jax.random.fold_in(streams_of[7], 71), 0),
        "slots": draw_slots(jax.random.fold_in(streams_of[7], 71), 0),
        "gate": jnp.clip(0.1 + 0.9 * jax.random.uniform(streams_of[4], (TOKENS,), jnp.float32) ** level_of(streams_of[4], (TOKENS,), ((0, 64),), -0.2, 0.2), 0.1, 1.0),
        "w_in": scatter_about(streams_of[5], (EXPERTS, D, FF), D ** -0.5, 0.125, ((0, 64), (2, 16))),
        "w_out": scatter_about(streams_of[6], (EXPERTS, FF, D), FF ** -0.5, 0.078125, ((0, 64), (1, 16))),
    }


def gelu_slope(pre_act):
    coeff = 0.7978845608
    tanh_part = jnp.tanh(coeff * (pre_act + 0.044715 * pre_act * pre_act * pre_act))
    return 0.5 * (1.0 + tanh_part) + 0.5 * pre_act * (1.0 - tanh_part * tanh_part) * coeff * (1.0 + 3.0 * 0.044715 * pre_act * pre_act)


def reference(tokens, cotangent, expert_ids, slots, gate, w_in, w_out):
    groups = TOKENS // TOK_DEV
    slot_total = EXPERTS * groups * CAP
    group_index = (jnp.arange(TOKENS) // TOK_DEV).astype(jnp.int32)
    target = jnp.where(slots >= 0, expert_ids * (groups * CAP) + group_index * CAP + slots, slot_total).astype(jnp.int32)
    scaled = (gate[:, None] * cotangent.astype(jnp.float32)).astype(jnp.bfloat16)
    blank_rows = jnp.zeros((slot_total + 1, D), jnp.bfloat16)
    dispatched_in = blank_rows.at[target].set(tokens)[:slot_total].reshape(EXPERTS, groups * CAP, D)
    dispatched_grad = blank_rows.at[target].set(scaled)[:slot_total].reshape(EXPERTS, groups * CAP, D)

    def one_expert(operands):
        inputs, grads, weights_in, weights_out = operands
        pre_act = jnp.dot(inputs, weights_in, preferred_element_type=jnp.float32)
        inner_grad = jnp.dot(grads, weights_out.T, preferred_element_type=jnp.float32)
        hidden_grad = (inner_grad * gelu_slope(pre_act)).astype(jnp.bfloat16)
        return jnp.dot(hidden_grad, weights_in.T, preferred_element_type=jnp.float32).astype(jnp.bfloat16)

    expert_grad = lax.map(one_expert, (dispatched_in, dispatched_grad, w_in, w_out))
    flat_grad = jnp.concatenate([expert_grad.reshape(slot_total, D), jnp.zeros((1, D), jnp.bfloat16)], axis=0)
    return flat_grad[target]
```

```python
import functools

import jax
import jax.numpy as jnp
from jax import lax
from jax.experimental import pallas as pl
from jax.experimental.pallas import tpu as pltpu
from jax.sharding import PartitionSpec as P

MESH = pl.DeviceIdType.MESH
F32 = jnp.float32
BF16 = jnp.bfloat16
CAP = 4
XH = 2
XL = 4


def gelu_slope(pre_act):
    coeff = 0.7978845608
    square = pre_act * pre_act
    tanh_part = jnp.tanh(coeff * (pre_act + 0.044715 * square * pre_act))
    return 0.5 * (1.0 + tanh_part) + 0.5 * pre_act * (1.0 - tanh_part * tanh_part) * coeff * (
        1.0 + 3.0 * 0.044715 * square
    )


def dot(a, b, dims=((1,), (0,))):
    return lax.dot_general(a, b, (dims, ((), ())), preferred_element_type=F32)


def kernel(
    XL, Y, ZC,
    tok_ref, cot_ref, ids_ref, slots_ref, gate_ref, win_hbm, wout_hbm,
    out_ref,
    win, wout, s1, r1, s2, g, pre, inner, hg, pf, u, q, fin, back, eg, s4, r4,
    wsem, z1s, z1r, x1s, x1r, ys, yr, rs, rr, x2s, x2r, z2s, z2r,
):
    X = XH * XL
    H = Y // 2
    tokens, feat = tok_ref.shape
    rows = ZC * CAP
    total = XL * rows
    span = XL * CAP

    expert = lax.axis_index("expert")
    mp = lax.axis_index("mp")
    x_lo, zc = lax.div(expert, ZC), lax.rem(expert, ZC)
    x_hi, y = lax.div(mp, Y), lax.rem(mp, Y)
    x = x_hi * XL + x_lo

    def at_zc(j):
        return (x_lo * ZC + lax.rem(zc + j, ZC), mp)

    def at_x(j):
        px = lax.rem(x + j, X)
        return (lax.rem(px, XL) * ZC + zc, lax.div(px, XL) * Y + y)

    def at_y(j):
        return (expert, x_hi * Y + lax.rem(y + Y + j, Y))

    loads = []
    for h in range(XH):
        loads.append(pltpu.make_async_copy(win_hbm.at[h], win.at[:, h], wsem.at[len(loads)]))
        for k in range(Y):
            loads.append(
                pltpu.make_async_copy(
                    wout_hbm.at[:, pl.ds((h * Y + k) * feat, feat)], wout.at[k, h], wsem.at[len(loads)]
                )
            )
    for load in loads:
        load.start()

    barrier = pltpu.get_barrier_semaphore()
    peers = [at_zc(j) for j in range(1, ZC)] + [at_x(j) for j in range(1, X)] + [at_y(1), at_y(-1)]
    for peer in peers:
        pl.semaphore_signal(barrier, inc=1, device_id=peer, device_id_type=MESH)

    ids, slots = ids_ref[...], slots_ref[...]
    target = jnp.where(
        slots >= 0, lax.rem(ids, ZC) * span + lax.div(ids, ZC) * CAP + slots, total
    )
    onehot = jnp.where(
        lax.broadcasted_iota(jnp.int32, (total, tokens), 0) == target, 1.0, 0.0
    ).astype(BF16)
    eye = lax.broadcasted_iota(jnp.int32, (tokens, tokens), 0) == lax.broadcasted_iota(
        jnp.int32, (tokens, tokens), 1
    )
    gate = jnp.sum(jnp.where(eye, gate_ref[...], 0.0), axis=1, keepdims=True)
    scaled = (gate * cot_ref[...].astype(F32)).astype(BF16)
    s1[0] = dot(onehot, tok_ref[...]).astype(BF16)
    s1[1] = dot(onehot, scaled).astype(BF16)

    pl.semaphore_wait(barrier, len(peers))

    def zc_rows(j):
        return pl.ds(pl.multiple_of(lax.rem(zc + j, ZC) * span, span), span)

    sends = []

    def send(src, dst, ssem, rsem, dev):
        copy = pltpu.make_async_remote_copy(
            src_ref=src, dst_ref=dst, send_sem=ssem, recv_sem=rsem, device_id=dev, device_id_type=MESH
        )
        copy.start()
        sends.append(copy)

    def arrive(dst, ssem, rsem, dev):
        pltpu.make_async_remote_copy(
            src_ref=dst, dst_ref=dst, send_sem=ssem, recv_sem=rsem, device_id=dev, device_id_type=MESH
        ).wait_recv()

    for j in range(1, ZC):
        send(s1.at[:, zc_rows(j)], r1.at[:, zc_rows(0)], z1s.at[j], z1r.at[j], at_zc(j))
    r1[:, zc_rows(0)] = s1[:, zc_rows(0)]

    ro = lax.broadcasted_iota(jnp.int32, (total, total), 0)
    ri = lax.broadcasted_iota(jnp.int32, (total, total), 1)
    ro_in = (
        lax.rem(lax.div(ro, CAP), ZC) * span + lax.div(ro, rows) * CAP + lax.rem(ro, CAP)
    )
    perm = jnp.where(ro_in == ri, 1.0, 0.0).astype(BF16)

    for j in range(1, ZC):
        arrive(r1.at[:, zc_rows(ZC - j)], z1s.at[j], z1r.at[j], at_zc(j))
    for t in range(2):
        s2[t] = dot(perm, r1[t]).astype(BF16).reshape(XL, rows, feat)

    order = [XL] + [j for d in range(1, XL) for j in (X - d, XL - d)]
    for j in order:
        px = lax.rem(x + j, X)
        send(
            s2.at[:, lax.rem(px, XL)], g.at[:, y, x_lo, x_hi], x1s.at[j], x1r.at[j], at_x(j)
        )
    g[:, y, x_lo, x_hi] = s2[:, x_lo]

    hops = ((H, H - 1), (H - 1, H))
    step = (1, -1)

    def ring_send(way, t, hop, c):
        yb = lax.rem(y + Y - step[way] * (hop - 1), Y)
        ref = g.at[t, yb, c]
        send(ref, ref, ys.at[way, t, hop - 1, c], yr.at[way, t, hop - 1, c], at_y(step[way]))

    def ring_arrive(way, t, hop, c):
        yb = lax.rem(y + Y - step[way] * hop, Y)
        arrive(
            g.at[t, yb, c], ys.at[way, t, hop - 1, c], yr.at[way, t, hop - 1, c], at_y(step[way])
        )

    def block(t, yb):
        return jnp.concatenate(
            [jnp.concatenate([g[t, yb, c, h] for h in range(XH)], axis=1) for c in range(XL)], axis=0
        )

    def weights(ref, yb, axis):
        return jnp.concatenate([ref[yb, h] for h in range(XH)], axis=axis)

    def accumulate(yb, first=False):
        a = dot(block(0, yb), weights(win, yb, 0))
        b = dot(block(1, yb), weights(wout, yb, 1), ((1,), (1,)))
        if first:
            pre[...], inner[...] = a, b
        else:
            pre[...] += a
            inner[...] += b

    chunks = [lax.rem(x_lo + d, XL) for d in range(XL)]
    for d in range(XL):
        for j in ([XL] if d == 0 else [X - d, XL - d]):
            src = lax.rem(x + X - j, X)
            arrive(
                g.at[:, y, lax.rem(src, XL), lax.div(src, XL)], x1s.at[j], x1r.at[j], at_x(j)
            )
        for t in range(2):
            for way in range(2):
                ring_send(way, t, 1, chunks[d])
    for load in loads:
        load.wait()
    accumulate(y, True)
    for hop in range(1, H + 1):
        for c in chunks:
            for t in range(2):
                for way in range(2):
                    if hop <= hops[way][t]:
                        ring_arrive(way, t, hop, c)
                        if hop < hops[way][t]:
                            ring_send(way, t, hop + 1, c)
        accumulate(lax.rem(y + hop, Y))
        if hop < H:
            accumulate(lax.rem(y + Y - hop, Y))

    hg[...] = (inner[...] * gelu_slope(pre[...])).astype(BF16)

    halves = (range(XL // 2), range(XL // 2, XL))
    start = ((H, H - 1), (H - 1, H))

    def partial(slot, yb):
        value = dot(hg[...], weights(win, yb, 0), ((1,), (1,)))
        for c in range(XL):
            for h in range(XH):
                pf[slot, c, h] = value[c * rows:(c + 1) * rows, h * feat:(h + 1) * feat]

    def sum_send(way, half, k, slot):
        for c in halves[half]:
            if k < start[way][half]:
                arrive(q.at[way, k, c], rs.at[way, k, c], rr.at[way, k, c], at_y(step[way]))
                u[way, k - 1, c] = (pf[slot, c] + q[way, k, c].astype(F32)).astype(BF16)
            else:
                u[way, k - 1, c] = pf[slot, c].astype(BF16)
            send(
                u.at[way, k - 1, c], q.at[way, k - 1, c], rs.at[way, k - 1, c], rr.at[way, k - 1, c],
                at_y(step[way]),
            )

    partial(0, lax.rem(y + H, Y))
    sum_send(0, 0, H, 0)
    sum_send(1, 1, H, 0)
    for k in range(H - 1, 0, -1):
        partial(2 * k - 1, lax.rem(y + k, Y))
        partial(2 * k, lax.rem(y + Y - k, Y))
        sum_send(0, 1, k, 2 * k - 1)
        sum_send(1, 0, k, 2 * k)
        sum_send(0, 0, k, 2 * k - 1)
        sum_send(1, 1, k, 2 * k)
    partial(0, y)
    for c in range(XL):
        value = pf[0, c]
        for way in range(2):
            arrive(q.at[way, 0, c], rs.at[way, 0, c], rr.at[way, 0, c], at_y(step[way]))
            value += q[way, 0, c].astype(F32)
        fin[c] = value.astype(BF16)

    for j in order:
        px = lax.rem(x + j, X)
        send(fin.at[lax.rem(px, XL), lax.div(px, XL)], back.at[j], x2s.at[j], x2r.at[j], at_x(j))
    back[0] = fin[x_lo, x_hi]
    for j in range(XL):
        for k in (j, j + XL):
            if k:
                arrive(back.at[k], x2s.at[k], x2r.at[k], at_x(k))
        eg[lax.rem(x_lo + XL - j, XL)] = (
            back[j].astype(F32) + back[j + XL].astype(F32)
        ).astype(BF16)
    s4[...] = dot(perm, eg[...].reshape(total, feat), ((0,), (0,))).astype(BF16)

    for j in range(1, ZC):
        send(s4.at[zc_rows(j)], r4.at[zc_rows(0)], z2s.at[j], z2r.at[j], at_zc(j))
    r4[zc_rows(0)] = s4[zc_rows(0)]
    for j in range(1, ZC):
        arrive(r4.at[zc_rows(ZC - j)], z2s.at[j], z2r.at[j], at_zc(j))
    out_ref[...] = dot(onehot, r4[...], ((0,), (0,))).astype(BF16)
    for copy in sends:
        copy.wait_send()


def local(XL, Y, ZC, tokens, cotangent, expert_ids, slots, gate, w_in, w_out):
    count, feat = tokens.shape
    hidden = w_in.shape[2]
    H = Y // 2
    rows = ZC * CAP
    total = XL * rows
    vmem = pl.BlockSpec(memory_space=pltpu.VMEM)
    hbm = pl.BlockSpec(memory_space=pl.ANY)
    dma = pltpu.SemaphoreType.DMA
    return pl.pallas_call(
        functools.partial(kernel, XL, Y, ZC),
        out_shape=jax.ShapeDtypeStruct((count, feat), BF16),
        in_specs=[vmem] * 5 + [hbm] * 2,
        out_specs=vmem,
        scratch_shapes=[
            pltpu.VMEM((Y, XH, feat, hidden), BF16),
            pltpu.VMEM((Y, XH, hidden, feat), BF16),
            pltpu.VMEM((2, total, feat), BF16),
            pltpu.VMEM((2, total, feat), BF16),
            pltpu.VMEM((2, XL, rows, feat), BF16),
            pltpu.VMEM((2, Y, XL, XH, rows, feat), BF16),
            pltpu.VMEM((total, hidden), F32),
            pltpu.VMEM((total, hidden), F32),
            pltpu.VMEM((total, hidden), BF16),
            pltpu.VMEM((2 * H - 1, XL, XH, rows, feat), F32),
            pltpu.VMEM((2, H, XL, XH, rows, feat), BF16),
            pltpu.VMEM((2, H, XL, XH, rows, feat), BF16),
            pltpu.VMEM((XL, XH, rows, feat), BF16),
            pltpu.VMEM((XH * XL, rows, feat), BF16),
            pltpu.VMEM((XL, rows, feat), BF16),
            pltpu.VMEM((total, feat), BF16),
            pltpu.VMEM((total, feat), BF16),
            dma((XH * (Y + 1),)),
            dma((ZC,)), dma((ZC,)),
            dma((XH * XL,)), dma((XH * XL,)),
            dma((2, 2, H, XL)), dma((2, 2, H, XL)),
            dma((2, H, XL)), dma((2, H, XL)),
            dma((XH * XL,)), dma((XH * XL,)),
            dma((ZC,)), dma((ZC,)),
        ],
        compiler_params=pltpu.CompilerParams(
            collective_id=0, has_side_effects=True, vmem_limit_bytes=40 * 1024 * 1024
        ),
        cost_estimate=pl.CostEstimate(
            flops=6 * total * w_in.shape[1] * hidden,
            bytes_accessed=4 * w_in.shape[1] * hidden,
            transcendentals=total * hidden,
        ),
    )(
        tokens,
        cotangent,
        expert_ids.reshape(1, count),
        slots.reshape(1, count),
        gate.reshape(1, count),
        w_in.reshape(XH, Y, feat, hidden),
        w_out.reshape(hidden, XH * Y * feat),
    )


def solution(mesh):
    in_specs = (
        P("expert", "mp"),
        P("expert", "mp"),
        P("expert"),
        P("expert"),
        P("expert"),
        P("expert", None, "mp"),
        P("expert", "mp", None),
    )
    return jax.shard_map(
        functools.partial(local, XL, mesh.shape["mp"] // XH, mesh.shape["expert"] // XL),
        mesh=mesh,
        in_specs=in_specs,
        out_specs=P("expert", "mp"),
        check_vma=False,
    )
```

```python
import functools

import jax
import jax.numpy as jnp
from jax import lax
from jax.experimental import pallas as pl
from jax.experimental.pallas import tpu as pltpu
from jax.sharding import PartitionSpec as P

MESH = pl.DeviceIdType.MESH
F32 = jnp.float32
BF16 = jnp.bfloat16
CAP = 4
WAVE = 4
GROUP = 2
VMEM_LIMIT = 63 * 1024 * 1024
XH = 2
XL = 4


def gelu_slope(pre_act):
    coeff = 0.7978845608
    square = pre_act * pre_act
    tanh_part = jnp.tanh(coeff * (pre_act + 0.044715 * square * pre_act))
    return 0.5 * (1.0 + tanh_part) + 0.5 * pre_act * (1.0 - tanh_part * tanh_part) * coeff * (
        1.0 + 3.0 * 0.044715 * square
    )


def dot(a, b, dims=((1,), (0,))):
    return lax.dot_general(a, b, (dims, ((), ())), preferred_element_type=F32)


def kernel(
    XL, Y, ZC,
    tok_hbm, cot_hbm, ids_hbm, slots_hbm, gate_hbm, win_hbm, wout_hbm,
    out_ref,
    tok_ref, cot_ref, ids_ref, slots_ref, gate_ref,
    win, wout, s1, r1, s2, g, pre, inner, hg, pf, u, q, fin, back, eg, s4, r4,
    isem, wsem, ssem, z1r, x1r, yr, rr, x2r, z2r,
):
    X = XH * XL
    H = Y // 2
    tokens, feat = tok_hbm.shape
    rows = ZC * CAP
    total = XL * rows
    span = XL * CAP

    expert = lax.axis_index("expert")
    mp = lax.axis_index("mp")
    x_lo, zc = lax.div(expert, ZC), lax.rem(expert, ZC)
    x_hi, y = lax.div(mp, Y), lax.rem(mp, Y)
    x = x_hi * XL + x_lo

    def at_zc(j):
        return (x_lo * ZC + lax.rem(zc + j, ZC), mp)

    def at_x(j):
        px = lax.rem(x + j, X)
        return (lax.rem(px, XL) * ZC + zc, lax.div(px, XL) * Y + y)

    def at_y(j):
        return (expert, x_hi * Y + lax.rem(y + Y + j, Y))

    def unit(j):
        px = lax.rem(x + X + j, X)
        return lax.rem(px, XL) * XH + lax.div(px, XL)

    def send(src, dst, sems, rsem, dev):
        pltpu.make_async_remote_copy(
            src_ref=src, dst_ref=dst, send_sem=sems, recv_sem=rsem, device_id=dev, device_id_type=MESH
        ).start()

    def arrive(dst, sems, rsem, dev):
        pltpu.make_async_remote_copy(
            src_ref=dst, dst_ref=dst, send_sem=sems, recv_sem=rsem, device_id=dev, device_id_type=MESH
        ).wait_recv()

    def sent(src, sems, dev):
        pltpu.make_async_remote_copy(
            src_ref=src, dst_ref=src, send_sem=sems, recv_sem=sems, device_id=dev, device_id_type=MESH
        ).wait_send()

    small = []
    for src, dst in (
        (ids_hbm, ids_ref), (slots_hbm, slots_ref), (gate_hbm, gate_ref), (tok_hbm, tok_ref), (cot_hbm, cot_ref)
    ):
        small.append(pltpu.make_async_copy(src, dst, isem.at[len(small)]))
        small[-1].start()

    barrier = pltpu.get_barrier_semaphore()
    peers = [at_zc(j) for j in range(1, ZC)] + [at_x(j) for j in range(1, X)] + [at_y(1), at_y(-1)]
    for peer in peers:
        pl.semaphore_signal(barrier, inc=1, device_id=peer, device_id_type=MESH)

    loads = []
    for h in range(XH):
        loads.append(pltpu.make_async_copy(win_hbm.at[h], win.at[:, h], wsem.at[len(loads)]))
        for k in range(Y):
            loads.append(
                pltpu.make_async_copy(
                    wout_hbm.at[:, pl.ds((h * Y + k) * feat, feat)], wout.at[k, h], wsem.at[len(loads)]
                )
            )
    for load in small:
        load.wait()

    ids, slots = ids_ref[...], slots_ref[...]
    target = jnp.where(
        slots >= 0, lax.rem(ids, ZC) * span + lax.div(ids, ZC) * CAP + slots, total
    )
    onehot = jnp.where(
        lax.broadcasted_iota(jnp.int32, (total, tokens), 0) == target, 1.0, 0.0
    ).astype(BF16)
    eye = lax.broadcasted_iota(jnp.int32, (tokens, tokens), 0) == lax.broadcasted_iota(
        jnp.int32, (tokens, tokens), 1
    )
    gate = jnp.sum(jnp.where(eye, gate_ref[...], 0.0), axis=1, keepdims=True)
    scaled = (gate * cot_ref[...].astype(F32)).astype(BF16)
    s1[0] = dot(onehot, tok_ref[...]).astype(BF16)
    s1[1] = dot(onehot, scaled).astype(BF16)

    pl.semaphore_wait(barrier, len(peers))

    def zc_rows(j):
        return pl.ds(pl.multiple_of(lax.rem(zc + j, ZC) * span, span), span)

    others = pl.ds(0, total - span)
    for j in range(1, ZC):
        send(s1.at[:, zc_rows(j)], r1.at[:, zc_rows(0)], ssem.at[0], z1r.at[0], at_zc(j))
    r1[:, zc_rows(0)] = s1[:, zc_rows(0)]
    for load in loads:
        load.start()

    ro = lax.broadcasted_iota(jnp.int32, (total, total), 0)
    ri = lax.broadcasted_iota(jnp.int32, (total, total), 1)
    ro_in = (
        lax.rem(lax.div(ro, CAP), ZC) * span + lax.div(ro, rows) * CAP + lax.rem(ro, CAP)
    )
    perm = jnp.where(ro_in == ri, 1.0, 0.0).astype(BF16)

    arrive(r1.at[:, others], ssem.at[0], z1r.at[0], at_zc(1))
    for t in range(2):
        s2[t] = dot(perm, r1[t]).astype(BF16).reshape(XL, rows, feat)

    near = sorted(range(X), key=lambda j: min(j, X - j))
    for j in near[1:]:
        px = lax.rem(x + j, X)
        send(s2.at[:, lax.rem(px, XL)], g.at[:, y, unit(0)], ssem.at[1], x1r.at[j], at_x(j))
    g[:, y, unit(0)] = s2[:, x_lo]

    step = (1, -1)

    def ring(way, hop, j, forward):
        yb = lax.rem(y + Y - step[way] * (hop - forward), Y)
        ref = g.at[way, yb, unit(-j)] if hop == H else g.at[:, yb, unit(-j)]
        args = (ref, ssem.at[2], yr.at[way, hop - 1, j], at_y(step[way]))
        if forward:
            send(ref, *args)
        else:
            arrive(*args)

    def block(t, yb):
        return jnp.concatenate(
            [jnp.concatenate([g[t, yb, c * XH + h] for h in range(XH)], axis=1) for c in range(XL)], axis=0
        )

    def weights(ref, yb, axis):
        return jnp.concatenate([ref[yb, h] for h in range(XH)], axis=axis)

    def accumulate(yb, first=False):
        a = dot(block(0, yb), weights(win, yb, 0))
        b = dot(block(1, yb), weights(wout, yb, 1), ((1,), (1,)))
        if first:
            pre[...], inner[...] = a, b
        else:
            pre[...] += a
            inner[...] += b

    waves = [near[i:i + WAVE] for i in range(0, X, WAVE)]
    for j in near:
        if j:
            arrive(g.at[:, y, unit(-j)], ssem.at[1], x1r.at[j], at_x(j))
        for way in range(2):
            ring(way, 1, j, 1)
    for hop in range(1, H + 1):
        for wave in waves:
            for j in wave:
                for way in range(2):
                    ring(way, hop, j, 0)
                    if hop < H:
                        ring(way, hop + 1, j, 1)
            if hop == 1 and wave is waves[0]:
                for load in loads:
                    load.wait()
                accumulate(y, True)
        accumulate(lax.rem(y + hop, Y))
        if hop < H:
            accumulate(lax.rem(y + Y - hop, Y))

    hg[...] = (inner[...] * gelu_slope(pre[...])).astype(BF16)

    far = near[::-1]
    groups = range(0, X, GROUP)

    def partial(slot, yb):
        value = dot(hg[...], weights(win, yb, 0), ((1,), (1,)))
        for c in range(XL):
            for h in range(XH):
                pf[slot, c * XH + h] = value[c * rows:(c + 1) * rows, h * feat:(h + 1) * feat]

    def landed(way, k, p):
        arrive(
            q.at[way, k, pl.ds(p, GROUP)], ssem.at[3], rr.at[way, k, p // GROUP], at_y(step[way])
        )

    def sum_send(first, k, slot):
        for p in groups:
            way = (p // GROUP + (not first)) % 2
            fresh = k == (H if first else H - 1)
            if not fresh:
                landed(way, k, p)
            for i in range(p, p + GROUP):
                value = pf[slot + way * (k < H), unit(far[i])]
                if not fresh:
                    value += q[way, k, i].astype(F32)
                u[way, k - 1, i] = value.astype(BF16)
            send(
                u.at[way, k - 1, pl.ds(p, GROUP)], q.at[way, k - 1, pl.ds(p, GROUP)],
                ssem.at[3], rr.at[way, k - 1, p // GROUP], at_y(step[way]),
            )

    def partials(k):
        for way in range(2):
            partial(2 * k - 1 + way, lax.rem(y + Y + step[way] * k, Y))

    partial(2 * H - 1, lax.rem(y + H, Y))
    sum_send(True, H, 2 * H - 1)
    for k in range(H - 1, 0, -1):
        partials(k)
        sum_send(False, k, 2 * k - 1)
        sum_send(True, k, 2 * k - 1)
    partial(0, y)
    for p in groups:
        for way in range(2):
            landed(way, 0, p)
        for i in range(p, p + GROUP):
            j = far[i]
            value = (
                pf[0, unit(j)] + q[0, 0, i].astype(F32) + q[1, 0, i].astype(F32)
            ).astype(BF16)
            if j:
                fin[i] = value
                send(fin.at[i], back.at[j], ssem.at[4], x2r.at[j], at_x(j))
            else:
                back[0] = value

    for j in range(XL):
        for k in (j, j + XL):
            if k:
                arrive(back.at[k], ssem.at[4], x2r.at[k], at_x(k))
        eg[lax.rem(x_lo + XL - j, XL)] = (
            back[j].astype(F32) + back[j + XL].astype(F32)
        ).astype(BF16)
    s4[...] = dot(perm, eg[...].reshape(total, feat), ((0,), (0,))).astype(BF16)

    for j in range(1, ZC):
        send(s4.at[zc_rows(j)], r4.at[zc_rows(0)], ssem.at[5], z2r.at[0], at_zc(j))
    r4[zc_rows(0)] = s4[zc_rows(0)]
    sent(s1.at[:, others], ssem.at[0], at_zc(1))
    sent(g.at[:, 0, pl.ds(0, X - 1)], ssem.at[1], at_x(1))
    sent(g.at[:, pl.ds(0, Y - 1)], ssem.at[2], at_y(1))
    sent(u.at[:, :, pl.ds(0, X * (Y - 1) // Y)], ssem.at[3], at_y(1))
    sent(fin.at[pl.ds(0, X - 1)], ssem.at[4], at_x(1))
    arrive(r4.at[others], ssem.at[5], z2r.at[0], at_zc(1))
    out_ref[...] = dot(onehot, r4[...], ((0,), (0,))).astype(BF16)
    sent(s4.at[others], ssem.at[5], at_zc(1))


def local(XL, Y, ZC, tokens, cotangent, expert_ids, slots, gate, w_in, w_out):
    count, feat = tokens.shape
    hidden = w_in.shape[2]
    X, H = XH * XL, Y // 2
    rows = ZC * CAP
    total = XL * rows
    vmem = pl.BlockSpec(memory_space=pltpu.VMEM)
    hbm = pl.BlockSpec(memory_space=pl.ANY)
    dma = pltpu.SemaphoreType.DMA
    return pl.pallas_call(
        functools.partial(kernel, XL, Y, ZC),
        out_shape=jax.ShapeDtypeStruct((count, feat), BF16),
        in_specs=[hbm] * 7,
        out_specs=vmem,
        scratch_shapes=[
            pltpu.VMEM((count, feat), BF16),
            pltpu.VMEM((count, feat), BF16),
            pltpu.VMEM((1, count), jnp.int32),
            pltpu.VMEM((1, count), jnp.int32),
            pltpu.VMEM((1, count), F32),
            pltpu.VMEM((Y, XH, feat, hidden), BF16),
            pltpu.VMEM((Y, XH, hidden, feat), BF16),
            pltpu.VMEM((2, total, feat), BF16),
            pltpu.VMEM((2, total, feat), BF16),
            pltpu.VMEM((2, XL, rows, feat), BF16),
            pltpu.VMEM((2, Y, X, rows, feat), BF16),
            pltpu.VMEM((total, hidden), F32),
            pltpu.VMEM((total, hidden), F32),
            pltpu.VMEM((total, hidden), BF16),
            pltpu.VMEM((Y, X, rows, feat), F32),
            pltpu.VMEM((2, H, X, rows, feat), BF16),
            pltpu.VMEM((2, H, X, rows, feat), BF16),
            pltpu.VMEM((X, rows, feat), BF16),
            pltpu.VMEM((X, rows, feat), BF16),
            pltpu.VMEM((XL, rows, feat), BF16),
            pltpu.VMEM((total, feat), BF16),
            pltpu.VMEM((total, feat), BF16),
            dma((5,)),
            dma((XH * (Y + 1),)),
            dma((6,)),
            dma((1,)),
            dma((X,)),
            dma((2, H, X)),
            dma((2, H, X // GROUP)),
            dma((X,)),
            dma((1,)),
        ],
        compiler_params=pltpu.CompilerParams(
            collective_id=0, has_side_effects=True, vmem_limit_bytes=VMEM_LIMIT
        ),
        cost_estimate=pl.CostEstimate(
            flops=6 * total * w_in.shape[1] * hidden,
            bytes_accessed=4 * w_in.shape[1] * hidden,
            transcendentals=total * hidden,
        ),
    )(
        tokens,
        cotangent,
        expert_ids.reshape(1, count),
        slots.reshape(1, count),
        gate.reshape(1, count),
        w_in.reshape(XH, Y, feat, hidden),
        w_out.reshape(hidden, XH * Y * feat),
    )


def solution(mesh):
    in_specs = (
        P("expert", "mp"),
        P("expert", "mp"),
        P("expert"),
        P("expert"),
        P("expert"),
        P("expert", None, "mp"),
        P("expert", "mp", None),
    )
    return jax.shard_map(
        functools.partial(local, XL, mesh.shape["mp"] // XH, mesh.shape["expert"] // XL),
        mesh=mesh,
        in_specs=in_specs,
        out_specs=P("expert", "mp"),
        check_vma=False,
    )
```

```python
import functools

import jax
import jax.numpy as jnp
from jax import lax
from jax.experimental import pallas as pl
from jax.experimental.pallas import tpu as pltpu
from jax.sharding import PartitionSpec as P

MESH = pl.DeviceIdType.MESH
F32 = jnp.float32
BF16 = jnp.bfloat16
CAP = 4
EARLY = {2: ((0, 1),), 4: ((1, 1), (2, 1)), 6: ((3, 1), (4, 1), (0, 2))}
GROUP = 2
VMEM_LIMIT = 63 * 1024 * 1024
XH = 2
XL = 4


def gelu_slope(pre_act):
    coeff = 0.7978845608
    square = pre_act * pre_act
    tanh_part = jnp.tanh(coeff * (pre_act + 0.044715 * square * pre_act))
    return 0.5 * (1.0 + tanh_part) + 0.5 * pre_act * (1.0 - tanh_part * tanh_part) * coeff * (
        1.0 + 3.0 * 0.044715 * square
    )


def dot(a, b, dims=((1,), (0,))):
    return lax.dot_general(a, b, (dims, ((), ())), preferred_element_type=F32)


def kernel(
    XL, Y, ZC,
    tok_hbm, cot_hbm, ids_hbm, slots_hbm, gate_hbm, win_hbm, wout_hbm,
    out_ref,
    tok_ref, cot_ref, ids_ref, slots_ref, gate_ref,
    win, wout, s1, r1, s2, g, pre, inner, hg, pf, u, q, fin, back, eg, s4, r4,
    isem, wsem, ssem, z1r, x1r, yr, rr, x2r, z2r,
):
    X = XH * XL
    H = Y // 2
    tokens, feat = tok_hbm.shape
    rows = ZC * CAP
    total = XL * rows
    span = XL * CAP

    expert = lax.axis_index("expert")
    mp = lax.axis_index("mp")
    x_lo, zc = lax.div(expert, ZC), lax.rem(expert, ZC)
    x_hi, y = lax.div(mp, Y), lax.rem(mp, Y)
    x = x_hi * XL + x_lo

    def at_zc(j):
        return (x_lo * ZC + lax.rem(zc + j, ZC), mp)

    def at_x(j):
        px = lax.rem(x + j, X)
        return (lax.rem(px, XL) * ZC + zc, lax.div(px, XL) * Y + y)

    def at_y(j):
        return (expert, x_hi * Y + lax.rem(y + Y + j, Y))

    def unit(j):
        px = lax.rem(x + X + j, X)
        return lax.rem(px, XL) * XH + lax.div(px, XL)

    def send(src, dst, sems, rsem, dev):
        pltpu.make_async_remote_copy(
            src_ref=src, dst_ref=dst, send_sem=sems, recv_sem=rsem, device_id=dev, device_id_type=MESH
        ).start()

    def arrive(dst, sems, rsem, dev):
        pltpu.make_async_remote_copy(
            src_ref=dst, dst_ref=dst, send_sem=sems, recv_sem=rsem, device_id=dev, device_id_type=MESH
        ).wait_recv()

    def sent(src, sems, dev):
        pltpu.make_async_remote_copy(
            src_ref=src, dst_ref=src, send_sem=sems, recv_sem=sems, device_id=dev, device_id_type=MESH
        ).wait_send()

    small = []
    for src, dst in (
        (ids_hbm, ids_ref), (slots_hbm, slots_ref), (gate_hbm, gate_ref), (tok_hbm, tok_ref), (cot_hbm, cot_ref)
    ):
        small.append(pltpu.make_async_copy(src, dst, isem.at[len(small)]))
        small[-1].start()

    barrier = pltpu.get_barrier_semaphore()
    peers = [at_zc(j) for j in range(1, ZC)] + [at_x(j) for j in range(1, X)] + [at_y(1), at_y(-1)]
    for peer in peers:
        pl.semaphore_signal(barrier, inc=1, device_id=peer, device_id_type=MESH)

    loads = []
    for h in range(XH):
        loads.append(pltpu.make_async_copy(win_hbm.at[h], win.at[:, h], wsem.at[len(loads)]))
        for k in range(Y):
            loads.append(
                pltpu.make_async_copy(
                    wout_hbm.at[:, pl.ds((h * Y + k) * feat, feat)], wout.at[k, h], wsem.at[len(loads)]
                )
            )
    for load in small:
        load.wait()

    ids, slots = ids_ref[...], slots_ref[...]
    target = jnp.where(
        slots >= 0, lax.rem(ids, ZC) * span + lax.div(ids, ZC) * CAP + slots, total
    )
    onehot = jnp.where(
        lax.broadcasted_iota(jnp.int32, (total, tokens), 0) == target, 1.0, 0.0
    ).astype(BF16)
    eye = lax.broadcasted_iota(jnp.int32, (tokens, tokens), 0) == lax.broadcasted_iota(
        jnp.int32, (tokens, tokens), 1
    )
    gate = jnp.sum(jnp.where(eye, gate_ref[...], 0.0), axis=1, keepdims=True)
    scaled = (gate * cot_ref[...].astype(F32)).astype(BF16)
    s1[0] = dot(onehot, tok_ref[...]).astype(BF16)
    s1[1] = dot(onehot, scaled).astype(BF16)

    pl.semaphore_wait(barrier, len(peers))

    def zc_rows(j):
        return pl.ds(pl.multiple_of(lax.rem(zc + j, ZC) * span, span), span)

    others = pl.ds(0, total - span)
    outward = sorted(range(1, ZC), key=lambda j: -min(j, ZC - j))
    for j in outward:
        send(s1.at[:, zc_rows(j)], r1.at[:, zc_rows(0)], ssem.at[0], z1r.at[0], at_zc(j))
    r1[:, zc_rows(0)] = s1[:, zc_rows(0)]
    for load in loads:
        load.start()

    ro = lax.broadcasted_iota(jnp.int32, (total, total), 0)
    ri = lax.broadcasted_iota(jnp.int32, (total, total), 1)
    ro_in = (
        lax.rem(lax.div(ro, CAP), ZC) * span + lax.div(ro, rows) * CAP + lax.rem(ro, CAP)
    )
    perm = jnp.where(ro_in == ri, 1.0, 0.0).astype(BF16)

    arrive(r1.at[:, others], ssem.at[0], z1r.at[0], at_zc(1))
    for t in range(2):
        s2[t] = dot(perm, r1[t]).astype(BF16).reshape(XL, rows, feat)

    near = sorted(range(X), key=lambda j: min(j, X - j))
    for j in near[1:]:
        px = lax.rem(x + j, X)
        send(s2.at[:, lax.rem(px, XL)], g.at[:, y, unit(0)], ssem.at[1], x1r.at[j], at_x(j))
    g[:, y, unit(0)] = s2[:, x_lo]

    step = (1, -1)

    def ring(way, hop, j, forward):
        yb = lax.rem(y + Y - step[way] * (hop - forward), Y)
        ref = g.at[way, yb, unit(-j)] if hop == H else g.at[:, yb, unit(-j)]
        args = (ref, ssem.at[2], yr.at[way, hop - 1, j], at_y(step[way]))
        if forward:
            send(ref, *args)
        else:
            arrive(*args)

    def block(t, yb):
        return jnp.concatenate(
            [jnp.concatenate([g[t, yb, c * XH + h] for h in range(XH)], axis=1) for c in range(XL)], axis=0
        )

    def weights(ref, yb, axis):
        return jnp.concatenate([ref[yb, h] for h in range(XH)], axis=axis)

    def accumulate(yb, first=False):
        a = dot(block(0, yb), weights(win, yb, 0))
        b = dot(block(1, yb), weights(wout, yb, 1), ((1,), (1,)))
        if first:
            pre[...], inner[...] = a, b
        else:
            pre[...] += a
            inner[...] += b

    passed = set()

    def pass_on(j, hop):
        if (j, hop) in passed:
            return
        passed.add((j, hop))
        for way in range(2):
            ring(way, hop, j, 0)
            if hop < H:
                ring(way, hop + 1, j, 1)

    for n, j in enumerate(near):
        if j:
            arrive(g.at[:, y, unit(-j)], ssem.at[1], x1r.at[j], at_x(j))
        for way in range(2):
            ring(way, 1, j, 1)
        for k, hop in EARLY.get(n, ()):
            pass_on(near[k], hop)
    for hop in range(1, H + 1):
        for n, j in enumerate(near):
            pass_on(j, hop)
            if hop == 1 and n == X // 2:
                for load in loads:
                    load.wait()
                accumulate(y, True)
        accumulate(lax.rem(y + hop, Y))
        if hop < H:
            accumulate(lax.rem(y + Y - hop, Y))

    hg[...] = (inner[...] * gelu_slope(pre[...])).astype(BF16)

    far = near[::-1]
    groups = range(0, X, GROUP)

    def partial(slot, yb):
        value = dot(hg[...], weights(win, yb, 0), ((1,), (1,)))
        for c in range(XL):
            for h in range(XH):
                pf[slot, c * XH + h] = value[c * rows:(c + 1) * rows, h * feat:(h + 1) * feat]

    def landed(way, k, p):
        arrive(
            q.at[way, k, pl.ds(p, GROUP)], ssem.at[3], rr.at[way, k, p // GROUP], at_y(step[way])
        )

    def sum_send(first, k, slot):
        for p in groups:
            way = (p // GROUP + (not first)) % 2
            fresh = k == (H if first else H - 1)
            if not fresh:
                landed(way, k, p)
            for i in range(p, p + GROUP):
                value = pf[slot + way * (k < H), unit(far[i])]
                if not fresh:
                    value += q[way, k, i].astype(F32)
                u[way, k - 1, i] = value.astype(BF16)
            send(
                u.at[way, k - 1, pl.ds(p, GROUP)], q.at[way, k - 1, pl.ds(p, GROUP)],
                ssem.at[3], rr.at[way, k - 1, p // GROUP], at_y(step[way]),
            )

    def partials(k):
        for way in range(2):
            partial(2 * k - 1 + way, lax.rem(y + Y + step[way] * k, Y))

    partial(2 * H - 1, lax.rem(y + H, Y))
    sum_send(True, H, 2 * H - 1)
    for k in range(H - 1, 0, -1):
        partials(k)
        sum_send(False, k, 2 * k - 1)
        sum_send(True, k, 2 * k - 1)
    partial(0, y)
    for p in groups:
        for way in range(2):
            landed(way, 0, p)
        for i in range(p, p + GROUP):
            j = far[i]
            value = (
                pf[0, unit(j)] + q[0, 0, i].astype(F32) + q[1, 0, i].astype(F32)
            ).astype(BF16)
            if j:
                fin[i] = value
                send(fin.at[i], back.at[j], ssem.at[4], x2r.at[j], at_x(j))
            else:
                back[0] = value

    for j in range(XL):
        for k in (j, j + XL):
            if k:
                arrive(back.at[k], ssem.at[4], x2r.at[k], at_x(k))
        eg[lax.rem(x_lo + XL - j, XL)] = (
            back[j].astype(F32) + back[j + XL].astype(F32)
        ).astype(BF16)
    s4[...] = dot(perm, eg[...].reshape(total, feat), ((0,), (0,))).astype(BF16)

    for j in outward:
        send(s4.at[zc_rows(j)], r4.at[zc_rows(0)], ssem.at[5], z2r.at[0], at_zc(j))
    r4[zc_rows(0)] = s4[zc_rows(0)]
    sent(s1.at[:, others], ssem.at[0], at_zc(1))
    sent(g.at[:, 0, pl.ds(0, X - 1)], ssem.at[1], at_x(1))
    sent(g.at[:, pl.ds(0, Y - 1)], ssem.at[2], at_y(1))
    sent(u.at[:, :, pl.ds(0, X * (Y - 1) // Y)], ssem.at[3], at_y(1))
    sent(fin.at[pl.ds(0, X - 1)], ssem.at[4], at_x(1))
    arrive(r4.at[others], ssem.at[5], z2r.at[0], at_zc(1))
    out_ref[...] = dot(onehot, r4[...], ((0,), (0,))).astype(BF16)
    sent(s4.at[others], ssem.at[5], at_zc(1))


def local(XL, Y, ZC, tokens, cotangent, expert_ids, slots, gate, w_in, w_out):
    count, feat = tokens.shape
    hidden = w_in.shape[2]
    X, H = XH * XL, Y // 2
    rows = ZC * CAP
    total = XL * rows
    vmem = pl.BlockSpec(memory_space=pltpu.VMEM)
    hbm = pl.BlockSpec(memory_space=pl.ANY)
    dma = pltpu.SemaphoreType.DMA
    return pl.pallas_call(
        functools.partial(kernel, XL, Y, ZC),
        out_shape=jax.ShapeDtypeStruct((count, feat), BF16),
        in_specs=[hbm] * 7,
        out_specs=vmem,
        scratch_shapes=[
            pltpu.VMEM((count, feat), BF16),
            pltpu.VMEM((count, feat), BF16),
            pltpu.VMEM((1, count), jnp.int32),
            pltpu.VMEM((1, count), jnp.int32),
            pltpu.VMEM((1, count), F32),
            pltpu.VMEM((Y, XH, feat, hidden), BF16),
            pltpu.VMEM((Y, XH, hidden, feat), BF16),
            pltpu.VMEM((2, total, feat), BF16),
            pltpu.VMEM((2, total, feat), BF16),
            pltpu.VMEM((2, XL, rows, feat), BF16),
            pltpu.VMEM((2, Y, X, rows, feat), BF16),
            pltpu.VMEM((total, hidden), F32),
            pltpu.VMEM((total, hidden), F32),
            pltpu.VMEM((total, hidden), BF16),
            pltpu.VMEM((Y, X, rows, feat), F32),
            pltpu.VMEM((2, H, X, rows, feat), BF16),
            pltpu.VMEM((2, H, X, rows, feat), BF16),
            pltpu.VMEM((X, rows, feat), BF16),
            pltpu.VMEM((X, rows, feat), BF16),
            pltpu.VMEM((XL, rows, feat), BF16),
            pltpu.VMEM((total, feat), BF16),
            pltpu.VMEM((total, feat), BF16),
            dma((5,)),
            dma((XH * (Y + 1),)),
            dma((6,)),
            dma((1,)),
            dma((X,)),
            dma((2, H, X)),
            dma((2, H, X // GROUP)),
            dma((X,)),
            dma((1,)),
        ],
        compiler_params=pltpu.CompilerParams(
            collective_id=0, has_side_effects=True, vmem_limit_bytes=VMEM_LIMIT
        ),
        cost_estimate=pl.CostEstimate(
            flops=6 * total * w_in.shape[1] * hidden,
            bytes_accessed=4 * w_in.shape[1] * hidden,
            transcendentals=total * hidden,
        ),
    )(
        tokens,
        cotangent,
        expert_ids.reshape(1, count),
        slots.reshape(1, count),
        gate.reshape(1, count),
        w_in.reshape(XH, Y, feat, hidden),
        w_out.reshape(hidden, XH * Y * feat),
    )


def solution(mesh):
    in_specs = (
        P("expert", "mp"),
        P("expert", "mp"),
        P("expert"),
        P("expert"),
        P("expert"),
        P("expert", None, "mp"),
        P("expert", "mp", None),
    )
    return jax.shard_map(
        functools.partial(local, XL, mesh.shape["mp"] // XH, mesh.shape["expert"] // XL),
        mesh=mesh,
        in_specs=in_specs,
        out_specs=P("expert", "mp"),
        check_vma=False,
    )
```

```python
import functools

import jax
import jax.numpy as jnp
from jax import lax
from jax.experimental import pallas as pl
from jax.experimental.pallas import tpu as pltpu
from jax.sharding import PartitionSpec as P

MESH = pl.DeviceIdType.MESH
F32 = jnp.float32
BF16 = jnp.bfloat16
CAP = 4
EARLY = {2: ((0, 1),), 4: ((1, 1), (2, 1)), 6: ((3, 1), (4, 1), (0, 2))}
GROUP = 2
VMEM_LIMIT = 63 * 1024 * 1024
XH = 2
XL = 4


def gelu_slope(pre_act):
    coeff = 0.7978845608
    square = pre_act * pre_act
    tanh_part = jnp.tanh(coeff * (pre_act + 0.044715 * square * pre_act))
    return 0.5 * (1.0 + tanh_part) + 0.5 * pre_act * (1.0 - tanh_part * tanh_part) * coeff * (
        1.0 + 3.0 * 0.044715 * square
    )


def dot(a, b, dims=((1,), (0,))):
    return lax.dot_general(a, b, (dims, ((), ())), preferred_element_type=F32)


def kernel(
    XL, Y, ZC,
    tok_hbm, cot_hbm, ids_hbm, slots_hbm, gate_hbm, win_hbm, wout_hbm,
    out_ref,
    tok_ref, cot_ref, ids_ref, slots_ref, gate_ref,
    win, wout, s1, r1, s2, g, pre, inner, hg, pf, u, q, fin, back, eg, s4, r4,
    isem, wsem, ssem, z1r, x1r, yr, rr, x2r, z2r,
):
    X = XH * XL
    H = Y // 2
    tokens, feat = tok_hbm.shape
    rows = ZC * CAP
    total = XL * rows
    span = XL * CAP

    expert = lax.axis_index("expert")
    mp = lax.axis_index("mp")
    x_lo, zc = lax.div(expert, ZC), lax.rem(expert, ZC)
    x_hi, y = lax.div(mp, Y), lax.rem(mp, Y)
    x = x_hi * XL + x_lo

    def at_zc(j):
        return (x_lo * ZC + lax.rem(zc + j, ZC), mp)

    def at_x(j):
        px = lax.rem(x + j, X)
        return (lax.rem(px, XL) * ZC + zc, lax.div(px, XL) * Y + y)

    def at_y(j):
        return (expert, x_hi * Y + lax.rem(y + Y + j, Y))

    def unit(j):
        px = lax.rem(x + X + j, X)
        return lax.rem(px, XL) * XH + lax.div(px, XL)

    def send(src, dst, sems, rsem, dev):
        pltpu.make_async_remote_copy(
            src_ref=src, dst_ref=dst, send_sem=sems, recv_sem=rsem, device_id=dev, device_id_type=MESH
        ).start()

    def arrive(dst, sems, rsem, dev):
        pltpu.make_async_remote_copy(
            src_ref=dst, dst_ref=dst, send_sem=sems, recv_sem=rsem, device_id=dev, device_id_type=MESH
        ).wait_recv()

    def sent(src, sems, dev):
        pltpu.make_async_remote_copy(
            src_ref=src, dst_ref=src, send_sem=sems, recv_sem=sems, device_id=dev, device_id_type=MESH
        ).wait_send()

    small = []
    for src, dst in (
        (ids_hbm, ids_ref), (slots_hbm, slots_ref), (gate_hbm, gate_ref), (tok_hbm, tok_ref), (cot_hbm, cot_ref)
    ):
        small.append(pltpu.make_async_copy(src, dst, isem.at[len(small)]))
        small[-1].start()

    barrier = pltpu.get_barrier_semaphore()
    peers = [at_zc(j) for j in range(1, ZC)] + [at_x(j) for j in range(1, X)] + [at_y(1), at_y(-1)]
    for peer in peers:
        pl.semaphore_signal(barrier, inc=1, device_id=peer, device_id_type=MESH)

    loads = []
    for h in range(XH):
        loads.append(pltpu.make_async_copy(win_hbm.at[h], win.at[:, h], wsem.at[len(loads)]))
        for k in range(Y):
            loads.append(
                pltpu.make_async_copy(
                    wout_hbm.at[:, pl.ds((h * Y + k) * feat, feat)], wout.at[k, h], wsem.at[len(loads)]
                )
            )
    for load in small:
        load.wait()

    ids, slots = ids_ref[...], slots_ref[...]
    target = jnp.where(
        slots >= 0, lax.rem(ids, ZC) * span + lax.div(ids, ZC) * CAP + slots, total
    )
    onehot = jnp.where(
        lax.broadcasted_iota(jnp.int32, (total, tokens), 0) == target, 1.0, 0.0
    ).astype(BF16)
    eye = lax.broadcasted_iota(jnp.int32, (tokens, tokens), 0) == lax.broadcasted_iota(
        jnp.int32, (tokens, tokens), 1
    )
    gate = jnp.sum(jnp.where(eye, gate_ref[...], 0.0), axis=1, keepdims=True)
    scaled = (gate * cot_ref[...].astype(F32)).astype(BF16)
    s1[0] = dot(onehot, tok_ref[...]).astype(BF16)
    s1[1] = dot(onehot, scaled).astype(BF16)

    pl.semaphore_wait(barrier, len(peers))

    def zc_rows(j):
        return pl.ds(pl.multiple_of(lax.rem(zc + j, ZC) * span, span), span)

    others = pl.ds(0, total - span)
    outward = sorted(range(1, ZC), key=lambda j: -min(j, ZC - j))
    for j in outward:
        send(s1.at[:, zc_rows(j)], r1.at[:, zc_rows(0)], ssem.at[0], z1r.at[0], at_zc(j))
    r1[:, zc_rows(0)] = s1[:, zc_rows(0)]
    for load in loads:
        load.start()

    ro = lax.broadcasted_iota(jnp.int32, (total, total), 0)
    ri = lax.broadcasted_iota(jnp.int32, (total, total), 1)
    ro_in = (
        lax.rem(lax.div(ro, CAP), ZC) * span + lax.div(ro, rows) * CAP + lax.rem(ro, CAP)
    )
    perm = jnp.where(ro_in == ri, 1.0, 0.0).astype(BF16)

    arrive(r1.at[:, others], ssem.at[0], z1r.at[0], at_zc(1))
    for t in range(2):
        s2[t] = dot(perm, r1[t]).astype(BF16).reshape(XL, rows, feat)

    near = sorted(range(X), key=lambda j: min(j, X - j))
    for j in near[1:]:
        px = lax.rem(x + j, X)
        send(s2.at[:, lax.rem(px, XL)], g.at[:, y, unit(0)], ssem.at[1], x1r.at[j], at_x(j))
    g[:, y, unit(0)] = s2[:, x_lo]

    step = (1, -1)

    def ring(way, hop, j, forward):
        yb = lax.rem(y + Y - step[way] * (hop - forward), Y)
        ref = g.at[way, yb, unit(-j)] if hop == H else g.at[:, yb, unit(-j)]
        args = (ref, ssem.at[2], yr.at[way, hop - 1, j], at_y(step[way]))
        if forward:
            send(ref, *args)
        else:
            arrive(*args)

    def block(t, yb):
        return jnp.concatenate(
            [jnp.concatenate([g[t, yb, c * XH + h] for h in range(XH)], axis=1) for c in range(XL)], axis=0
        )

    def weights(ref, yb, axis):
        return jnp.concatenate([ref[yb, h] for h in range(XH)], axis=axis)

    def accumulate(yb, first=False):
        a = dot(block(0, yb), weights(win, yb, 0))
        b = dot(block(1, yb), weights(wout, yb, 1), ((1,), (1,)))
        if first:
            pre[...], inner[...] = a, b
        else:
            pre[...] += a
            inner[...] += b

    passed = set()

    def pass_on(j, hop):
        if (j, hop) in passed:
            return
        passed.add((j, hop))
        for way in range(2):
            ring(way, hop, j, 0)
            if hop < H:
                ring(way, hop + 1, j, 1)

    for n, j in enumerate(near):
        if j:
            arrive(g.at[:, y, unit(-j)], ssem.at[1], x1r.at[j], at_x(j))
        for way in range(2):
            ring(way, 1, j, 1)
        for k, hop in EARLY.get(n, ()):
            pass_on(near[k], hop)
    for hop in range(1, H + 1):
        for n, j in enumerate(near):
            pass_on(j, hop)
            if hop == 1 and n == X // 2:
                for load in loads:
                    load.wait()
                accumulate(y, True)
            elif hop > 1 and n == X // 4:
                accumulate(lax.rem(y + hop - 1, Y))
            elif hop > 1 and n == X - X // 4:
                accumulate(lax.rem(y + Y - hop + 1, Y))
    accumulate(lax.rem(y + H, Y))

    hg[...] = (inner[...] * gelu_slope(pre[...])).astype(BF16)

    far = near[::-1]
    groups = range(0, X, GROUP)

    def partial(slot, yb):
        value = dot(hg[...], weights(win, yb, 0), ((1,), (1,)))
        for c in range(XL):
            for h in range(XH):
                pf[slot, c * XH + h] = value[c * rows:(c + 1) * rows, h * feat:(h + 1) * feat]

    def landed(way, k, p):
        arrive(
            q.at[way, k, pl.ds(p, GROUP)], ssem.at[3], rr.at[way, k, p // GROUP], at_y(step[way])
        )

    def sum_send(first, k, slot):
        for p in groups:
            way = (p // GROUP + (not first)) % 2
            fresh = k == (H if first else H - 1)
            if not fresh:
                landed(way, k, p)
            for i in range(p, p + GROUP):
                value = pf[slot + way * (k < H), unit(far[i])]
                if not fresh:
                    value += q[way, k, i].astype(F32)
                u[way, k - 1, i] = value.astype(BF16)
            send(
                u.at[way, k - 1, pl.ds(p, GROUP)], q.at[way, k - 1, pl.ds(p, GROUP)],
                ssem.at[3], rr.at[way, k - 1, p // GROUP], at_y(step[way]),
            )

    def partials(k):
        for way in range(2):
            partial(2 * k - 1 + way, lax.rem(y + Y + step[way] * k, Y))

    partial(2 * H - 1, lax.rem(y + H, Y))
    sum_send(True, H, 2 * H - 1)
    for k in range(H - 1, 0, -1):
        partials(k)
        sum_send(False, k, 2 * k - 1)
        sum_send(True, k, 2 * k - 1)
    partial(0, y)
    for p in groups:
        for way in range(2):
            landed(way, 0, p)
        for i in range(p, p + GROUP):
            j = far[i]
            value = (
                pf[0, unit(j)] + q[0, 0, i].astype(F32) + q[1, 0, i].astype(F32)
            ).astype(BF16)
            if j:
                fin[i] = value
                send(fin.at[i], back.at[j], ssem.at[4], x2r.at[j], at_x(j))
            else:
                back[0] = value

    for j in range(XL):
        for k in (j, j + XL):
            if k:
                arrive(back.at[k], ssem.at[4], x2r.at[k], at_x(k))
        eg[lax.rem(x_lo + XL - j, XL)] = (
            back[j].astype(F32) + back[j + XL].astype(F32)
        ).astype(BF16)
    s4[...] = dot(perm, eg[...].reshape(total, feat), ((0,), (0,))).astype(BF16)

    for j in outward:
        send(s4.at[zc_rows(j)], r4.at[zc_rows(0)], ssem.at[5], z2r.at[0], at_zc(j))
    r4[zc_rows(0)] = s4[zc_rows(0)]
    sent(s1.at[:, others], ssem.at[0], at_zc(1))
    sent(g.at[:, 0, pl.ds(0, X - 1)], ssem.at[1], at_x(1))
    sent(g.at[:, pl.ds(0, Y - 1)], ssem.at[2], at_y(1))
    sent(u.at[:, :, pl.ds(0, X * (Y - 1) // Y)], ssem.at[3], at_y(1))
    sent(fin.at[pl.ds(0, X - 1)], ssem.at[4], at_x(1))
    arrive(r4.at[others], ssem.at[5], z2r.at[0], at_zc(1))
    out_ref[...] = dot(onehot, r4[...], ((0,), (0,))).astype(BF16)
    sent(s4.at[others], ssem.at[5], at_zc(1))


def local(XL, Y, ZC, tokens, cotangent, expert_ids, slots, gate, w_in, w_out):
    count, feat = tokens.shape
    hidden = w_in.shape[2]
    X, H = XH * XL, Y // 2
    rows = ZC * CAP
    total = XL * rows
    vmem = pl.BlockSpec(memory_space=pltpu.VMEM)
    hbm = pl.BlockSpec(memory_space=pl.ANY)
    dma = pltpu.SemaphoreType.DMA
    return pl.pallas_call(
        functools.partial(kernel, XL, Y, ZC),
        out_shape=jax.ShapeDtypeStruct((count, feat), BF16),
        in_specs=[hbm] * 7,
        out_specs=vmem,
        scratch_shapes=[
            pltpu.VMEM((count, feat), BF16),
            pltpu.VMEM((count, feat), BF16),
            pltpu.VMEM((1, count), jnp.int32),
            pltpu.VMEM((1, count), jnp.int32),
            pltpu.VMEM((1, count), F32),
            pltpu.VMEM((Y, XH, feat, hidden), BF16),
            pltpu.VMEM((Y, XH, hidden, feat), BF16),
            pltpu.VMEM((2, total, feat), BF16),
            pltpu.VMEM((2, total, feat), BF16),
            pltpu.VMEM((2, XL, rows, feat), BF16),
            pltpu.VMEM((2, Y, X, rows, feat), BF16),
            pltpu.VMEM((total, hidden), F32),
            pltpu.VMEM((total, hidden), F32),
            pltpu.VMEM((total, hidden), BF16),
            pltpu.VMEM((Y, X, rows, feat), F32),
            pltpu.VMEM((2, H, X, rows, feat), BF16),
            pltpu.VMEM((2, H, X, rows, feat), BF16),
            pltpu.VMEM((X, rows, feat), BF16),
            pltpu.VMEM((X, rows, feat), BF16),
            pltpu.VMEM((XL, rows, feat), BF16),
            pltpu.VMEM((total, feat), BF16),
            pltpu.VMEM((total, feat), BF16),
            dma((5,)),
            dma((XH * (Y + 1),)),
            dma((6,)),
            dma((1,)),
            dma((X,)),
            dma((2, H, X)),
            dma((2, H, X // GROUP)),
            dma((X,)),
            dma((1,)),
        ],
        compiler_params=pltpu.CompilerParams(
            collective_id=0, has_side_effects=True, vmem_limit_bytes=VMEM_LIMIT
        ),
        cost_estimate=pl.CostEstimate(
            flops=6 * total * w_in.shape[1] * hidden,
            bytes_accessed=4 * w_in.shape[1] * hidden,
            transcendentals=total * hidden,
        ),
    )(
        tokens,
        cotangent,
        expert_ids.reshape(1, count),
        slots.reshape(1, count),
        gate.reshape(1, count),
        w_in.reshape(XH, Y, feat, hidden),
        w_out.reshape(hidden, XH * Y * feat),
    )


def solution(mesh):
    in_specs = (
        P("expert", "mp"),
        P("expert", "mp"),
        P("expert"),
        P("expert"),
        P("expert"),
        P("expert", None, "mp"),
        P("expert", "mp", None),
    )
    return jax.shard_map(
        functools.partial(local, XL, mesh.shape["mp"] // XH, mesh.shape["expert"] // XL),
        mesh=mesh,
        in_specs=in_specs,
        out_specs=P("expert", "mp"),
        check_vma=False,
    )
```
